32 devices in a mesh: ctx: 16 (over z, x, core), tp: 2 (over y).
Axes of the slice: x: 2, y: 2, z: 4, core: 2. Of those that a mesh axis runs over, the one named last changes fastest.
Arguments:
- projected: bfloat16 [3, 4096, 8192], P(None, 'ctx', 'tp'), may hold values from -6 to 6
- short_weight: float32 [3, 3, 8192], P(None, None, 'tp'), may hold values from -4 to 4
- rate: float32 [8192, 16], P('tp'), may hold values from 0.00012207031 to 0.05
- residue: float32 [8192, 16], P('tp'), may hold values from -5 to 5
- skip: float32 [8192], P('tp'), may hold values from -4 to 4
- w_out: bfloat16 [8192, 4096], P('tp'), may hold values from -0.09375 to 0.09375
Outputs:
- layer_out: bfloat16 [4096, 4096], P('ctx', 'tp')
The draws below stay inside these ranges and needn't reach their ends.
All inputs are finite; a program needn't handle non-finite values.
Results may differ from the reference program's by a relative error of at most 0.011.
Values may be sent and summed in bfloat16 or wider, within the bound.
A program may use at most 256 MiB of HBM per device.

```python
import math
import jax
import jax.numpy as jnp
from jax import lax

D = 8192
OUTW = 4096
MODES = 16
TOK_DEV = 256
TOKENS = 4096
N_CTX = 16


def with_spikes(values, stream_key, source, target, blocks, factor):
    def block_of(position):
        return (jnp.arange(values.shape[position]) // (values.shape[position] // blocks)).reshape((-1,) + (1,) * (values.ndim - 1 - position))

    one_side = jax.random.permutation(stream_key, blocks)[block_of(target)]
    other_side = (block_of(target) + blocks // 2) % blocks
    return jnp.where((block_of(source) == one_side) | (block_of(source) == other_side), factor * values, values)


def shard_levels(key, shape, shards, smallest, top_value):
    gain = 1.0
    for dim, blocks in shards:
        steps = jax.random.uniform(jax.random.fold_in(jax.random.fold_in(key, 6), dim), (blocks,), jnp.float32, smallest / len(shards), top_value / len(shards))
        gain = gain * jnp.repeat(jnp.exp(steps), shape[dim] // blocks).reshape((-1,) + (1,) * (len(shape) - 1 - dim))
    return gain


def gaussian(own_key, shape, deviation, most, pieces=(), kind=jnp.bfloat16):
    loudness = shard_levels(own_key, shape, pieces, -0.22, 0.18) if pieces else 1.0
    values = jax.random.normal(own_key, shape, jnp.float32) * deviation * loudness
    return jnp.minimum(jnp.maximum(values, -most), most).astype(kind)


def noise_with(stream_key, extent, deviation, reach, shards, heavy, held_as=jnp.bfloat16):
    result = deviation * jax.random.normal(stream_key, extent, jnp.float32)
    if shards:
        result = result * shard_levels(stream_key, extent, shards, -0.22, 0.18)
    return jnp.clip(with_spikes(result, jax.random.fold_in(stream_key, 3), *heavy), -reach, reach).astype(held_as)


def setup_inputs(seed: int = 0) -> dict:
    splits = jax.random.split(jax.random.key(seed), 7)
    return {
        "projected": gaussian(splits[0], (3, TOKENS, D), 1.0, 6.0, ((1, 16), (2, 2))),
        "short_weight": gaussian(splits[1], (3, 3, D), 0.6, 4.0, ((2, 2),), jnp.float32),
        "rate": jnp.clip(jnp.exp(math.log(0.05) - 6.015181 * jax.random.uniform(splits[2], (D, MODES), jnp.float32) ** shard_levels(splits[2], (D, MODES), ((0, 2),), -0.2, 0.2)), 0.00012207031, 0.05),
        "residue": gaussian(splits[3], (D, MODES), 1.0, 5.0, ((0, 2),), jnp.float32),
        "skip": gaussian(splits[4], (D,), 1.0, 4.0, ((0, 2),), jnp.float32),
        "w_out": noise_with(splits[5], (D, OUTW), D ** -0.5, 0.09375, ((0, 2),), (0, 1, 2, 2.0)),
    }


two_pi = 2.0 * math.pi

def matmul_f32(form, left, right):
    return jnp.einsum(form, left.astype(jnp.float32), right.astype(jnp.float32))

def dft_tables(count_a, count_b):
    span_a = 2 * count_a
    freq_a = jnp.arange(span_a, dtype=jnp.int32)
    pos_a = jnp.arange(count_a, dtype=jnp.int32)
    pos_b = jnp.arange(count_b, dtype=jnp.int32)
    angle_a = two_pi / span_a * (freq_a[:, None] * pos_a[None, :] % span_a).astype(jnp.float32)
    angle_b = two_pi / count_b * (pos_b[:, None] * pos_b[None, :] % count_b).astype(jnp.float32)
    return (jnp.cos(angle_a).astype(jnp.bfloat16), jnp.sin(angle_a).astype(jnp.bfloat16), jnp.cos(angle_b).astype(jnp.bfloat16), jnp.sin(angle_b).astype(jnp.bfloat16))

def twist_tables(rows_k, cols_b, full_len):
    angle = two_pi / full_len * (rows_k[:, None] * cols_b[None, :] % full_len).astype(jnp.float32)
    return (jnp.cos(angle), jnp.sin(angle))

def filter_spectrum(frequency, rate, residue, length):
    full_len = 2 * length
    mode_count = rate.shape[1]
    steps_f = (frequency % full_len).astype(jnp.float32)
    half_sin = jnp.sin(math.pi / full_len * steps_f)[:, None]
    full_sin = jnp.sin(two_pi / full_len * steps_f)[:, None]
    parity = (1 - 2 * (frequency % 2)).astype(jnp.float32)[:, None]

    def add_mode(mode_index, partial_value):
        rates_now = lax.dynamic_index_in_dim(rate, mode_index, 1, keepdims=False)[None, :]
        mode_weight = lax.dynamic_index_in_dim(residue, mode_index, 1, keepdims=False)[None, :]
        damping = jnp.exp(-rates_now)
        denom_re = -jnp.expm1(-rates_now) + 2.0 * damping * half_sin * half_sin
        denom_im = damping * full_sin
        numerator = mode_weight * jnp.sqrt(2.0 * rates_now / mode_count) * (1.0 - jnp.exp(-rates_now * length) * parity)
        factor = numerator / (denom_re * denom_re + denom_im * denom_im)
        return (partial_value[0] + factor * denom_re, partial_value[1] - factor * denom_im)
    grid_shape = (frequency.shape[0], rate.shape[0])
    initial = (jnp.zeros(grid_shape, jnp.float32), jnp.zeros(grid_shape, jnp.float32))
    return lax.fori_loop(0, mode_count, add_mode, initial)

def reference(projected, short_weight, rate, residue, skip, w_out):
    count_a = N_CTX
    count_b = TOK_DEV
    length = count_a * count_b
    span_a = 2 * count_a
    full_len = span_a * count_b
    taps = short_weight.astype(jnp.float32)
    features = []
    for branch in range(3):
        padded = jnp.concatenate([jnp.zeros((2, D), jnp.bfloat16), projected[branch]], axis=0).astype(jnp.float32)
        mixed = taps[branch, 0][None, :] * padded[2:] + taps[branch, 1][None, :] * padded[1:-1] + taps[branch, 2][None, :] * padded[:-2]
        features.append(mixed.astype(jnp.bfloat16))
    query_feat, key_feat, value_feat = features
    product = (key_feat.astype(jnp.float32) * value_feat.astype(jnp.float32)).astype(jnp.bfloat16)
    cos_a, sin_a, cos_b, sin_b = dft_tables(count_a, count_b)
    twist_cos, twist_sin = twist_tables(jnp.arange(span_a, dtype=jnp.int32), jnp.arange(count_b, dtype=jnp.int32), full_len)
    twist_cos = twist_cos[:, :, None]
    twist_sin = twist_sin[:, :, None]
    frequency = (jnp.arange(span_a, dtype=jnp.int32)[:, None] + span_a * jnp.arange(count_b, dtype=jnp.int32)[None, :]).reshape(-1)
    block_size = min(D, 256)
    block_count = D // block_size

    def one_block(operands):
        prod_blk, rate_blk, resid_blk = operands
        inputs = prod_blk.reshape(count_a, count_b, block_size)
        real_part = matmul_f32('ka,abc->kbc', cos_a, inputs)
        imag_part = -matmul_f32('ka,abc->kbc', sin_a, inputs)
        section_re = (real_part * twist_cos + imag_part * twist_sin).astype(jnp.bfloat16)
        section_im = (imag_part * twist_cos - real_part * twist_sin).astype(jnp.bfloat16)
        spec_re = matmul_f32('kbc,bm->kmc', section_re, cos_b) + matmul_f32('kbc,bm->kmc', section_im, sin_b)
        spec_im = matmul_f32('kbc,bm->kmc', section_im, cos_b) - matmul_f32('kbc,bm->kmc', section_re, sin_b)
        resp_re, resp_im = filter_spectrum(frequency, rate_blk, resid_blk, length)
        resp_re = resp_re.reshape(span_a, count_b, block_size)
        resp_im = resp_im.reshape(span_a, count_b, block_size)
        filt_re = (spec_re * resp_re - spec_im * resp_im).astype(jnp.bfloat16)
        filt_im = (spec_re * resp_im + spec_im * resp_re).astype(jnp.bfloat16)
        back_re = matmul_f32('kmc,mb->kbc', filt_re, cos_b) - matmul_f32('kmc,mb->kbc', filt_im, sin_b)
        back_im = matmul_f32('kmc,mb->kbc', filt_re, sin_b) + matmul_f32('kmc,mb->kbc', filt_im, cos_b)
        twist_re = (back_re * twist_cos - back_im * twist_sin).astype(jnp.bfloat16)
        twist_im = (back_im * twist_cos + back_re * twist_sin).astype(jnp.bfloat16)
        summed = matmul_f32('ka,kbc->abc', cos_a, twist_re) - matmul_f32('ka,kbc->abc', sin_a, twist_im)
        return (summed * (1.0 / full_len)).astype(jnp.bfloat16).reshape(length, block_size)
    prod_blocks = product.reshape(length, block_count, block_size).transpose(1, 0, 2)
    rate_blocks = rate.reshape(block_count, block_size, MODES)
    resid_blocks = residue.reshape(block_count, block_size, MODES)
    convolved = lax.map(one_block, (prod_blocks, rate_blocks, resid_blocks))
    convolved = convolved.transpose(1, 0, 2).reshape(length, D)
    gated = (query_feat.astype(jnp.float32) * (convolved.astype(jnp.float32) + skip[None, :] * product.astype(jnp.float32))).astype(jnp.bfloat16)
    return jnp.dot(gated, w_out, preferred_element_type=jnp.float32).astype(jnp.bfloat16)
```

```python
import functools
import math

import jax
import jax.numpy as jnp
import numpy as np
from jax import lax
from jax.experimental import pallas as pl
from jax.experimental.pallas import tpu as pltpu
from jax.sharding import PartitionSpec as P

LANES = 128
SUB = 8


def half_tables(block):
    k = np.arange(block)[:, None]
    t = np.arange(block)[None, :]
    angle = np.pi / (2 * block) * ((2 * k + 1) * t % (4 * block))
    fwd = np.concatenate([np.cos(angle), np.sin(angle)], axis=0)
    return jnp.asarray(fwd, jnp.bfloat16), jnp.asarray(fwd.T, jnp.bfloat16)


def spread(ref, modes, lanes):
    return jnp.stack(
        [jnp.broadcast_to(ref[m : m + 1, lanes], (SUB, LANES)) for m in range(modes)]
    )


def mode_weight(rates, residues, modes):
    return residues * jnp.sqrt(2.0 * rates / modes)


def local_kernel(
    proj, halo, short, rate, residue, skip, fwd, inv, query, base, state, line, taps, prod
):
    tokens, width = proj.shape[1], proj.shape[2]
    modes = rate.shape[0]
    row = lax.broadcasted_iota(jnp.int32, (1, SUB, LANES), 1).astype(jnp.float32)
    for j in range(width // LANES):
        lanes = slice(j * LANES, (j + 1) * LANES)
        feats = []
        for s in range(3):
            now = proj[s, :, lanes].astype(jnp.float32)
            line[s, SUB - 2 : SUB, :] = halo[s, :, lanes].astype(jnp.float32)
            line[s, SUB : SUB + tokens, :] = now
            mixed = (
                short[s, 0:1, lanes] * now
                + short[s, 1:2, lanes] * line[s, SUB - 1 : SUB - 1 + tokens, :]
                + short[s, 2:3, lanes] * line[s, SUB - 2 : SUB - 2 + tokens, :]
            )
            feats.append(mixed.astype(jnp.bfloat16))
        query[:, lanes] = feats[0]
        product = (feats[1].astype(jnp.float32) * feats[2].astype(jnp.float32)).astype(jnp.bfloat16)
        prod[:, lanes] = product
        line[0, SUB : SUB + tokens, :] = product.astype(jnp.float32)

        rates = spread(rate, modes, lanes)
        weight = mode_weight(rates, spread(residue, modes, lanes), modes)
        step = jnp.exp(-SUB * rates)
        power = weight * jnp.exp(-rates * row)

        def advance(i, carry):
            power, held = carry
            rows = []
            for half in range(2):
                start = pl.multiple_of(SUB + i * 2 * SUB + half * SUB, SUB)
                held = held * step + line[0, pl.ds(start, SUB), :][None]
                rows.append(jnp.sum(power, axis=0))
                power = power * step
            at = pl.multiple_of(i * 2 * SUB, 2 * SUB)
            taps[pl.ds(at, 2 * SUB), lanes] = jnp.concatenate(rows, axis=0).astype(jnp.bfloat16)
            return power, held

        _, held = lax.fori_loop(
            0, tokens // (2 * SUB), advance, (power, jnp.zeros_like(power))
        )
        held = held * jnp.exp(-rates * (SUB - 1 - row))
        state[:, lanes] = jnp.sum(held, axis=1).astype(state.dtype)

    sig = jnp.dot(fwd[...], prod[...], preferred_element_type=jnp.float32)
    fil = jnp.dot(fwd[...], taps[...], preferred_element_type=jnp.float32)
    cs, ss, cf, sf = sig[:tokens], sig[tokens:], fil[:tokens], fil[tokens:]
    both = jnp.concatenate(
        [(cs * cf - ss * sf).astype(jnp.bfloat16), (cs * sf + ss * cf).astype(jnp.bfloat16)], axis=0
    )
    conv = jnp.dot(inv[...], both, preferred_element_type=jnp.float32) * (1.0 / tokens)
    base[...] = conv + skip[...] * prod[...].astype(jnp.float32)


def gate_kernel(query, base, enter, rate, residue, w_out, out, gated):
    tokens, channels = query.shape
    modes = rate.shape[0]

    @pl.when(pl.program_id(0) == 0)
    def _():
        row = lax.broadcasted_iota(jnp.int32, (1, SUB, LANES), 1).astype(jnp.float32)

        @pl.loop(0, channels // LANES)
        def _(j):
            lanes = pl.ds(pl.multiple_of(j * LANES, LANES), LANES)
            rates = spread(rate, modes, lanes)
            weight = mode_weight(rates, spread(residue, modes, lanes), modes)
            step = jnp.exp(-SUB * rates)
            power = weight * jnp.exp(-rates * (row + 1.0)) * spread(enter, modes, lanes)

            def advance(i, power):
                rows = []
                for half in range(2):
                    rows.append(jnp.sum(power, axis=0))
                    power = power * step
                at = pl.ds(pl.multiple_of(i * 2 * SUB, 2 * SUB), 2 * SUB)
                total = jnp.concatenate(rows, axis=0) + base[at, lanes]
                gated[at, lanes] = (query[at, lanes].astype(jnp.float32) * total).astype(
                    jnp.bfloat16
                )
                return power

            lax.fori_loop(0, tokens // (2 * SUB), advance, power)

    out[0] = jnp.dot(
        gated[...], w_out[...], preferred_element_type=jnp.float32
    ).astype(jnp.bfloat16)


def on_device(projected, short_weight, rate, residue, skip, w_out):
    count = lax.axis_size("ctx")
    parts = lax.axis_size("tp")
    rank = lax.axis_index("ctx")
    _, tokens, channels = projected.shape
    modes = rate.shape[1]
    outputs = w_out.shape[1]
    rate_t, residue_t = rate.T, residue.T
    halo = lax.ppermute(
        projected[:, -2:, :], "ctx", [(i, i + 1) for i in range(count - 1)]
    )
    fwd, inv = half_tables(tokens)
    width = min(512, channels)
    by_col = lambda *lead: pl.BlockSpec(lead + (width,), lambda i: (0,) * len(lead) + (i,))
    whole = lambda shape: pl.BlockSpec(shape, lambda i: (0,) * len(shape))
    query, base, state = pl.pallas_call(
        local_kernel,
        grid=(channels // width,),
        in_specs=[
            by_col(3, tokens), by_col(3, 2), by_col(3, 3), by_col(modes), by_col(modes),
            by_col(1), whole(fwd.shape), whole(inv.shape),
        ],
        out_specs=[by_col(tokens), by_col(tokens), by_col(modes)],
        out_shape=[
            jax.ShapeDtypeStruct((tokens, channels), jnp.bfloat16),
            jax.ShapeDtypeStruct((tokens, channels), jnp.float32),
            jax.ShapeDtypeStruct((modes, channels), jnp.float32),
        ],
        scratch_shapes=[
            pltpu.VMEM((3, tokens + SUB, LANES), jnp.float32),
            pltpu.VMEM((tokens, width), jnp.bfloat16),
            pltpu.VMEM((tokens, width), jnp.bfloat16),
        ],
        compiler_params=pltpu.CompilerParams(vmem_limit_bytes=40 * 2**20),
        name="local",
    )(projected, halo, short_weight, rate_t, residue_t, skip[None], fwd, inv)

    share = channels // count
    got = lax.all_to_all(
        state.astype(jnp.bfloat16).reshape(modes, count, share).transpose(1, 0, 2),
        "ctx", split_axis=0, concat_axis=0, tiled=True,
    ).astype(jnp.float32)
    decay = jnp.exp(-float(tokens) * lax.dynamic_slice_in_dim(rate_t, rank * share, share, 1))
    held = jnp.zeros((modes, share), jnp.float32)
    enter = []
    for i in range(count):
        enter.append(held)
        held = held * decay + got[i]
    enter = lax.all_to_all(
        jnp.stack(enter).astype(jnp.bfloat16), "ctx", split_axis=0, concat_axis=0, tiled=True
    )
    enter = enter.transpose(1, 0, 2).reshape(modes, channels).astype(jnp.float32)

    tile = min(512, outputs // parts)
    per = outputs // parts // tile
    summed = pl.pallas_call(
        gate_kernel,
        grid=(outputs // tile,),
        in_specs=[
            whole(query.shape), whole(base.shape), whole(enter.shape), whole(rate_t.shape),
            whole(rate_t.shape), pl.BlockSpec((channels, tile), lambda i: (0, i)),
        ],
        out_specs=pl.BlockSpec((1, tokens, tile), lambda i: (i // per, 0, i % per)),
        out_shape=jax.ShapeDtypeStruct((parts, tokens, outputs // parts), jnp.bfloat16),
        scratch_shapes=[pltpu.VMEM((tokens, channels), jnp.bfloat16)],
        compiler_params=pltpu.CompilerParams(vmem_limit_bytes=50 * 2**20),
        name="gate",
    )(query, base, enter, rate_t, residue_t, w_out)
    return lax.psum_scatter(summed, "tp", scatter_dimension=0, tiled=True)[0]


def solution(mesh):
    return jax.shard_map(
        on_device,
        mesh=mesh,
        in_specs=(
            P(None, "ctx", "tp"),
            P(None, None, "tp"),
            P("tp", None),
            P("tp", None),
            P("tp"),
            P("tp", None),
        ),
        out_specs=P("ctx", "tp"),
        check_vma=False,
    )
```

```python
import functools
import math

import jax
import jax.numpy as jnp
import numpy as np
from jax import lax
from jax.experimental import pallas as pl
from jax.experimental.pallas import tpu as pltpu
from jax.sharding import PartitionSpec as P

LANES = 128
SUB = 8
MESH = pl.DeviceIdType.MESH


def half_tables(block):
    k = np.arange(block)[:, None]
    t = np.arange(block)[None, :]
    angle = np.pi / (2 * block) * ((2 * k + 1) * t % (4 * block))
    fwd = np.concatenate([np.cos(angle), np.sin(angle)], axis=0)
    return jnp.asarray(fwd, jnp.bfloat16), jnp.asarray(fwd.T, jnp.bfloat16)


def spread(rows):
    return jnp.stack(
        [jnp.broadcast_to(rows[m : m + 1], (SUB, LANES)) for m in range(rows.shape[0])]
    )


def mode_weight(rates, residues, modes):
    return residues * jnp.sqrt(2.0 * rates / modes)


def local_kernel(
    proj, halo, short, rate, residue, skip, fwd, inv, query, base, state, line, taps, prod
):
    tokens, width = proj.shape[1], proj.shape[2]
    modes = rate.shape[1]
    row = lax.broadcasted_iota(jnp.int32, (1, SUB, LANES), 1).astype(jnp.float32)
    for j in range(width // LANES):
        lanes = slice(j * LANES, (j + 1) * LANES)
        feats = []
        for s in range(3):
            now = proj[s, :, lanes].astype(jnp.float32)
            line[s, SUB - 2 : SUB, :] = halo[s, :, lanes].astype(jnp.float32)
            line[s, SUB : SUB + tokens, :] = now
            mixed = (
                short[s, 0:1, lanes] * now
                + short[s, 1:2, lanes] * line[s, SUB - 1 : SUB - 1 + tokens, :]
                + short[s, 2:3, lanes] * line[s, SUB - 2 : SUB - 2 + tokens, :]
            )
            feats.append(mixed.astype(jnp.bfloat16))
        query[:, lanes] = feats[0]
        product = (feats[1].astype(jnp.float32) * feats[2].astype(jnp.float32)).astype(jnp.bfloat16)
        prod[:, lanes] = product
        line[0, SUB : SUB + tokens, :] = product.astype(jnp.float32)

        rates = spread(rate[j])
        weight = mode_weight(rates, spread(residue[j]), modes)
        step = jnp.exp(-SUB * rates)
        power = weight * jnp.exp(-rates * row)

        def advance(i, carry):
            power, held = carry
            rows = []
            for half in range(2):
                start = pl.multiple_of(SUB + i * 2 * SUB + half * SUB, SUB)
                held = held * step + line[0, pl.ds(start, SUB), :][None]
                rows.append(jnp.sum(power, axis=0))
                power = power * step
            at = pl.multiple_of(i * 2 * SUB, 2 * SUB)
            taps[pl.ds(at, 2 * SUB), lanes] = jnp.concatenate(rows, axis=0).astype(jnp.bfloat16)
            return power, held

        _, held = lax.fori_loop(
            0, tokens // (2 * SUB), advance, (power, jnp.zeros_like(power))
        )
        held = held * jnp.exp(-rates * (SUB - 1 - row))
        state[j] = jnp.sum(held, axis=1).astype(state.dtype)

    sig = jnp.dot(fwd[...], prod[...], preferred_element_type=jnp.float32)
    fil = jnp.dot(fwd[...], taps[...], preferred_element_type=jnp.float32)
    cs, ss, cf, sf = sig[:tokens], sig[tokens:], fil[:tokens], fil[tokens:]
    both = jnp.concatenate(
        [(cs * cf - ss * sf).astype(jnp.bfloat16), (cs * sf + ss * cf).astype(jnp.bfloat16)], axis=0
    )
    conv = jnp.dot(inv[...], both, preferred_element_type=jnp.float32) * (1.0 / tokens)
    base[...] = conv + skip[...] * prod[...].astype(jnp.float32)


def finish_kernel(
    state, query, base, rate, residue, decay_rate, w_out, out,
    w_buf, gated, got, enter_out, enter, send, recv, own,
    w_sem, s1, r1, s2, r2, s3, r3,
):
    tokens, channels = query.shape
    modes = rate.shape[1]
    count, share = state.shape[0], state.shape[1]
    parts, rank = lax.axis_size("tp"), lax.axis_index("ctx")
    me = lax.axis_index("tp")
    tiles, _, tile = w_buf.shape
    per = tiles // parts
    away = tiles - per

    def load(i):
        peer = lax.rem(me + 1 + i // per, parts)
        col = pl.multiple_of((peer * per + i % per) * tile, tile)
        return pltpu.make_async_copy(w_out.at[:, pl.ds(col, tile)], w_buf.at[i], w_sem.at[i])

    @pl.loop(0, tiles)
    def _(i):
        load(i).start()

    barrier = pltpu.get_barrier_semaphore()

    @pl.loop(1, count)
    def _(o):
        pl.semaphore_signal(
            barrier, inc=1, device_id=(lax.rem(rank + o, count), me), device_id_type=MESH
        )

    @pl.loop(1, parts)
    def _(o):
        pl.semaphore_signal(
            barrier, inc=1, device_id=(rank, lax.rem(me + o, parts)), device_id_type=MESH
        )

    pl.semaphore_wait(barrier, count + parts - 2)

    def hop(src, dst, peer, slot, sent, landed):
        return pltpu.make_async_remote_copy(
            src_ref=src.at[peer], dst_ref=dst.at[slot], send_sem=sent.at[peer],
            recv_sem=landed.at[slot], device_id=(peer, me), device_id_type=MESH,
        )

    @pl.loop(1, count)
    def _(o):
        hop(state, got, lax.rem(rank + o, count), rank, s1, r1).start()

    got[rank] = state[rank]

    @pl.loop(1, count)
    def _(o):
        peer = lax.rem(rank + o, count)
        hop(state, got, peer, peer, s1, r1).wait()

    decay = jnp.exp(-float(tokens) * decay_rate[rank])

    def prefix(i, held):
        enter_out[i] = held.astype(enter_out.dtype)
        return held * decay + got[i].astype(jnp.float32)

    lax.fori_loop(0, count, prefix, jnp.zeros((share, LANES), jnp.float32))

    @pl.loop(1, count)
    def _(o):
        hop(enter_out, enter, lax.rem(rank + o, count), rank, s2, r2).start()

    enter[rank] = enter_out[rank]

    @pl.loop(1, count)
    def _(o):
        peer = lax.rem(rank + o, count)
        hop(enter_out, enter, peer, peer, s2, r2).wait()

    row = lax.broadcasted_iota(jnp.int32, (1, SUB, LANES), 1).astype(jnp.float32)

    def entering(j):
        if share >= modes:
            fold = share // modes
            at = pl.multiple_of((j % fold) * modes, modes)
            return spread(enter[j // fold, pl.ds(at, modes), :].astype(jnp.float32))
        fold = modes // share
        return jnp.concatenate(
            [spread(enter[j * fold + i].astype(jnp.float32)) for i in range(fold)], axis=0
        )

    @pl.loop(0, channels // LANES)
    def _(j):
        lanes = pl.ds(pl.multiple_of(j * LANES, LANES), LANES)
        rates = spread(rate[j])
        weight = mode_weight(rates, spread(residue[j]), modes)
        step = jnp.exp(-SUB * rates)
        power = weight * jnp.exp(-rates * (row + 1.0)) * entering(j)

        def advance(i, power):
            rows = []
            for half in range(2):
                rows.append(jnp.sum(power, axis=0))
                power = power * step
            at = pl.ds(pl.multiple_of(i * 2 * SUB, 2 * SUB), 2 * SUB)
            total = jnp.concatenate(rows, axis=0) + base[at, lanes]
            gated[at, lanes] = (query[at, lanes].astype(jnp.float32) * total).astype(jnp.bfloat16)
            return power

        lax.fori_loop(0, tokens // (2 * SUB), advance, power)

    def product(i):
        load(i).wait()
        return jnp.dot(gated[...], w_buf[i], preferred_element_type=jnp.float32)

    def give(i):
        peer = lax.rem(me + 1 + i // per, parts)
        return pltpu.make_async_remote_copy(
            src_ref=send.at[i], dst_ref=recv.at[i], send_sem=s3.at[i], recv_sem=r3.at[i],
            device_id=(rank, peer), device_id_type=MESH,
        )

    @pl.loop(0, away)
    def _(i):
        send[i] = product(i).astype(jnp.bfloat16)
        give(i).start()

    @pl.loop(0, per)
    def _(t):
        own[t] = product(away + t)

    for t in range(per):
        total = own[t]
        for o in range(parts - 1):
            give(o * per + t).wait()
            total = total + recv[o * per + t].astype(jnp.float32)
        out[:, t * tile : (t + 1) * tile] = total.astype(out.dtype)


def on_device(projected, short_weight, rate, residue, skip, w_out):
    count = lax.axis_size("ctx")
    parts = lax.axis_size("tp")
    _, tokens, channels = projected.shape
    modes = rate.shape[1]
    outputs = w_out.shape[1]
    blocks = channels // LANES
    rate_b = rate.reshape(blocks, LANES, modes).transpose(0, 2, 1)
    residue_b = residue.reshape(blocks, LANES, modes).transpose(0, 2, 1)
    halo = lax.ppermute(
        projected[:, -2:, :], "ctx", [(i, i + 1) for i in range(count - 1)]
    )
    fwd, inv = half_tables(tokens)
    width = min(512, channels)
    by_col = lambda *lead: pl.BlockSpec(lead + (width,), lambda i: (0,) * len(lead) + (i,))
    by_block = pl.BlockSpec((width // LANES, modes, LANES), lambda i: (i, 0, 0))
    whole = lambda shape: pl.BlockSpec(shape, lambda i: (0,) * len(shape))
    query, base, state = pl.pallas_call(
        local_kernel,
        grid=(channels // width,),
        in_specs=[
            by_col(3, tokens), by_col(3, 2), by_col(3, 3), by_block, by_block,
            by_col(1), whole(fwd.shape), whole(inv.shape),
        ],
        out_specs=[by_col(tokens), by_col(tokens), by_block],
        out_shape=[
            jax.ShapeDtypeStruct((tokens, channels), jnp.bfloat16),
            jax.ShapeDtypeStruct((tokens, channels), jnp.float32),
            jax.ShapeDtypeStruct((blocks, modes, LANES), jnp.bfloat16),
        ],
        scratch_shapes=[
            pltpu.VMEM((3, tokens + SUB, LANES), jnp.float32),
            pltpu.VMEM((tokens, width), jnp.bfloat16),
            pltpu.VMEM((tokens, width), jnp.bfloat16),
        ],
        compiler_params=pltpu.CompilerParams(vmem_limit_bytes=40 * 2**20),
        name="local",
    )(projected, halo, short_weight, rate_b, residue_b, skip[None], fwd, inv)

    share = blocks * modes // count
    each = outputs // parts
    tile = min(512, each)
    tiles = outputs // tile
    away = tiles - each // tile
    vmem = pl.BlockSpec(memory_space=pltpu.VMEM)
    return pl.pallas_call(
        finish_kernel,
        in_specs=[vmem] * 6 + [pl.BlockSpec(memory_space=pl.ANY)],
        out_specs=vmem,
        out_shape=jax.ShapeDtypeStruct((tokens, each), jnp.bfloat16),
        scratch_shapes=[
            pltpu.VMEM((tiles, channels, tile), jnp.bfloat16),
            pltpu.VMEM((tokens, channels), jnp.bfloat16),
            pltpu.VMEM((count, share, LANES), jnp.bfloat16),
            pltpu.VMEM((count, share, LANES), jnp.bfloat16),
            pltpu.VMEM((count, share, LANES), jnp.bfloat16),
            pltpu.VMEM((away, tokens, tile), jnp.bfloat16),
            pltpu.VMEM((away, tokens, tile), jnp.bfloat16),
            pltpu.VMEM((each // tile, tokens, tile), jnp.float32),
            pltpu.SemaphoreType.DMA((tiles,)),
        ]
        + [pltpu.SemaphoreType.DMA((count,))] * 4
        + [pltpu.SemaphoreType.DMA((away,))] * 2,
        compiler_params=pltpu.CompilerParams(
            vmem_limit_bytes=56 * 2**20, collective_id=0, has_side_effects=True
        ),
        name="finish",
    )(
        state.reshape(count, share, LANES), query, base, rate_b, residue_b,
        rate_b.reshape(count, share, LANES), w_out,
    )


def solution(mesh):
    return jax.shard_map(
        on_device,
        mesh=mesh,
        in_specs=(
            P(None, "ctx", "tp"),
            P(None, None, "tp"),
            P("tp", None),
            P("tp", None),
            P("tp"),
            P("tp", None),
        ),
        out_specs=P("ctx", "tp"),
        check_vma=False,
    )
```

```python
import math

import jax
import jax.numpy as jnp
import numpy as np
from jax import lax
from jax.experimental import pallas as pl
from jax.experimental.pallas import tpu as pltpu
from jax.sharding import PartitionSpec as P

LANES = 128
SUB = 8
SPAN = 4
HALVES = 2
MESH = pl.DeviceIdType.MESH


def half_tables(block):
    k = np.arange(block)[:, None]
    t = np.arange(block)[None, :]
    angle = np.pi / (2 * block) * ((2 * k + 1) * t % (4 * block))
    fwd = np.concatenate([np.cos(angle), np.sin(angle)], axis=0)
    return jnp.asarray(fwd, jnp.bfloat16), jnp.asarray(fwd.T, jnp.bfloat16)


def spread(rows):
    return jnp.stack(
        [jnp.broadcast_to(rows[m : m + 1], (SUB, LANES)) for m in range(rows.shape[0])]
    )


def mode_weight(rates, residues, modes):
    return residues * jnp.sqrt(2.0 * rates / modes)


def fold(power):
    while power.shape[0] > 1 and power.shape[0] % 2 == 0:
        half = power.shape[0] // 2
        power = power[:half] + power[half:]
    return jnp.sum(power, axis=0)


def layer_kernel(
    proj, halo, short, rate, residue, skip, decay_rate, fwd, inv, w_out, out,
    w_buf, line, taps, prod, query, base, state, got, enter_out, enter, send, recv, own,
    w_sem, s1, r1, s2, r2, s3, r3,
):
    _, tokens, channels = proj.shape
    modes = rate.shape[1]
    count, share = got.shape[0], got.shape[1]
    parts, rank = lax.axis_size("tp"), lax.axis_index("ctx")
    me = lax.axis_index("tp")
    tiles, _, tile = w_buf.shape
    per = tiles // parts
    away = tiles - per
    width = taps.shape[1]
    group = SPAN * SUB
    row = lax.broadcasted_iota(jnp.int32, (1, SUB, LANES), 1).astype(jnp.float32)

    def load(i):
        peer = lax.rem(me + 1 + i // per, parts)
        col = pl.multiple_of((peer * per + i % per) * tile, tile)
        return pltpu.make_async_copy(w_out.at[:, pl.ds(col, tile)], w_buf.at[i], w_sem.at[i])

    @pl.loop(0, tiles)
    def _(i):
        load(i).start()

    barrier = pltpu.get_barrier_semaphore()

    @pl.loop(1, count)
    def _(o):
        pl.semaphore_signal(
            barrier, inc=1, device_id=(lax.rem(rank + o, count), me), device_id_type=MESH
        )

    @pl.loop(1, parts)
    def _(o):
        pl.semaphore_signal(
            barrier, inc=1, device_id=(rank, lax.rem(me + o, parts)), device_id_type=MESH
        )

    @pl.loop(0, channels // LANES)
    def _(j):
        lanes = pl.ds(pl.multiple_of(j * LANES, LANES), LANES)
        feats = []
        for s in range(3):
            now = proj[s, :, lanes].astype(jnp.float32)
            line[s, SUB - 2 : SUB, :] = halo[s, :, lanes].astype(jnp.float32)
            line[s, SUB : SUB + tokens, :] = now
            mixed = (
                short[s, 0:1, lanes] * now
                + short[s, 1:2, lanes] * line[s, SUB - 1 : SUB - 1 + tokens, :]
                + short[s, 2:3, lanes] * line[s, SUB - 2 : SUB - 2 + tokens, :]
            )
            feats.append(mixed.astype(jnp.bfloat16))
        query[:, lanes] = feats[0]
        product = (feats[1].astype(jnp.float32) * feats[2].astype(jnp.float32)).astype(jnp.bfloat16)
        prod[:, lanes] = product
        line[0, SUB : SUB + tokens, :] = product.astype(jnp.float32)
        rates = spread(rate[j])
        step = jnp.exp(-SUB * rates)

        def advance(i, held):
            for k in range(SPAN):
                start = pl.multiple_of(SUB + i * group + k * SUB, SUB)
                held = held * step + line[0, pl.ds(start, SUB), :][None]
            return held

        held = lax.fori_loop(0, tokens // group, advance, jnp.zeros((modes, SUB, LANES), jnp.float32))
        held = jnp.sum(held * jnp.exp(-rates * (SUB - 1 - row)), axis=1).astype(state.dtype)
        if share >= modes:
            times = share // modes
            at = pl.multiple_of((j % times) * modes, modes)
            state[j // times, pl.ds(at, modes), :] = held
        else:
            times = modes // share
            for i in range(times):
                state[j * times + i] = held[i * share : (i + 1) * share]

    pl.semaphore_wait(barrier, count + parts - 2)

    def inside(start, stop):
        @pl.loop(start, stop)
        def _(b):
            cols = pl.ds(pl.multiple_of(b * width, width), width)
            for n in range(width // LANES):
                j = b * (width // LANES) + n
                rates = spread(rate[j])
                weight = mode_weight(rates, spread(residue[j]), modes)
                step = jnp.exp(-SUB * rates)

                def advance(i, power):
                    rows = []
                    for _ in range(SPAN):
                        rows.append(fold(power))
                        power = power * step
                    at = pl.ds(pl.multiple_of(i * group, group), group)
                    taps[at, n * LANES : (n + 1) * LANES] = jnp.concatenate(rows, axis=0).astype(
                        jnp.bfloat16
                    )
                    return power

                lax.fori_loop(0, tokens // group, advance, weight * jnp.exp(-rates * row))
            here = prod[:, cols]
            sig = jnp.dot(fwd[...], here, preferred_element_type=jnp.float32)
            fil = jnp.dot(fwd[...], taps[...], preferred_element_type=jnp.float32)
            cs, ss, cf, sf = sig[:tokens], sig[tokens:], fil[:tokens], fil[tokens:]
            both = jnp.concatenate(
                [
                    (cs * cf - ss * sf).astype(jnp.bfloat16),
                    (cs * sf + ss * cf).astype(jnp.bfloat16),
                ],
                axis=0,
            )
            conv = jnp.dot(inv[...], both, preferred_element_type=jnp.float32) * (1.0 / tokens)
            base[:, cols] = conv + skip[:, cols] * here.astype(jnp.float32)

    pieces = channels // width
    def hop(src, dst, peer, slot, sent, landed):
        return pltpu.make_async_remote_copy(
            src_ref=src.at[peer], dst_ref=dst.at[slot], send_sem=sent.at[peer],
            recv_sem=landed.at[slot], device_id=(peer, me), device_id_type=MESH,
        )

    @pl.loop(1, count)
    def _(o):
        hop(state, got, lax.rem(rank + o, count), rank, s1, r1).start()

    got[rank] = state[rank]
    inside(0, pieces // 2)

    @pl.loop(1, count)
    def _(o):
        peer = lax.rem(rank + o, count)
        hop(state, got, peer, peer, s1, r1).wait()

    decay = jnp.exp(-float(tokens) * decay_rate[rank])

    def prefix(i, held):
        enter_out[i] = held.astype(enter_out.dtype)
        return held * decay + got[i].astype(jnp.float32)

    lax.fori_loop(0, count, prefix, jnp.zeros((share, LANES), jnp.float32))

    @pl.loop(1, count)
    def _(o):
        hop(enter_out, enter, lax.rem(rank + o, count), rank, s2, r2).start()

    enter[rank] = enter_out[rank]
    inside(pieces // 2, pieces)

    @pl.loop(1, count)
    def _(o):
        peer = lax.rem(rank + o, count)
        hop(enter_out, enter, peer, peer, s2, r2).wait()

    def entering(j):
        if share >= modes:
            times = share // modes
            at = pl.multiple_of((j % times) * modes, modes)
            return spread(enter[j // times, pl.ds(at, modes), :].astype(jnp.float32))
        times = modes // share
        return jnp.concatenate(
            [spread(enter[j * times + i].astype(jnp.float32)) for i in range(times)], axis=0
        )

    part = tokens // HALVES

    def gate(begin):
        @pl.loop(0, channels // LANES)
        def _(j):
            lanes = pl.ds(pl.multiple_of(j * LANES, LANES), LANES)
            rates = spread(rate[j])
            weight = mode_weight(rates, spread(residue[j]), modes)
            step = jnp.exp(-SUB * rates)

            def advance(i, power):
                rows = []
                for _ in range(SPAN):
                    rows.append(fold(power))
                    power = power * step
                at = pl.ds(pl.multiple_of(begin + i * group, group), group)
                total = jnp.concatenate(rows, axis=0) + base[at, lanes]
                query[at, lanes] = (query[at, lanes].astype(jnp.float32) * total).astype(
                    jnp.bfloat16
                )
                return power

            lax.fori_loop(
                0, part // group, advance,
                weight * jnp.exp(-rates * (row + (begin + 1.0))) * entering(j),
            )

    def give(i):
        peer = lax.rem(me + 1 + (i % away) // per, parts)
        return pltpu.make_async_remote_copy(
            src_ref=send.at[i], dst_ref=recv.at[i], send_sem=s3.at[i], recv_sem=r3.at[i],
            device_id=(rank, peer), device_id_type=MESH,
        )

    for h in range(HALVES):
        gate(h * part)

        @pl.loop(0, away)
        def _(i):
            if h == 0:
                load(i).wait()
            send[h * away + i] = jnp.dot(
                query[h * part : (h + 1) * part, :], w_buf[i], preferred_element_type=jnp.float32
            ).astype(jnp.bfloat16)
            give(h * away + i).start()

    @pl.loop(0, per)
    def _(t):
        load(away + t).wait()
        own[t] = jnp.dot(query[...], w_buf[away + t], preferred_element_type=jnp.float32)

    for h in range(HALVES):
        for t in range(per):
            total = own[t, h * part : (h + 1) * part, :]
            for o in range(parts - 1):
                give(h * away + o * per + t).wait()
                total = total + recv[h * away + o * per + t].astype(jnp.float32)
            out[h * part : (h + 1) * part, t * tile : (t + 1) * tile] = total.astype(out.dtype)


def on_device(projected, short_weight, rate, residue, skip, w_out):
    count = lax.axis_size("ctx")
    parts = lax.axis_size("tp")
    _, tokens, channels = projected.shape
    modes = rate.shape[1]
    outputs = w_out.shape[1]
    blocks = channels // LANES
    rate_b = rate.reshape(blocks, LANES, modes).transpose(0, 2, 1)
    residue_b = residue.reshape(blocks, LANES, modes).transpose(0, 2, 1)
    halo = lax.ppermute(
        projected[:, -2:, :], "ctx", [(i, i + 1) for i in range(count - 1)]
    )
    fwd, inv = half_tables(tokens)
    width = min(512, channels)
    share = blocks * modes // count
    each = outputs // parts
    tile = min(512, each)
    tiles = outputs // tile
    away = tiles - each // tile
    vmem = pl.BlockSpec(memory_space=pltpu.VMEM)
    return pl.pallas_call(
        layer_kernel,
        in_specs=[vmem] * 9 + [pl.BlockSpec(memory_space=pl.ANY)],
        out_specs=vmem,
        out_shape=jax.ShapeDtypeStruct((tokens, each), jnp.bfloat16),
        scratch_shapes=[
            pltpu.VMEM((tiles, channels, tile), jnp.bfloat16),
            pltpu.VMEM((3, tokens + SUB, LANES), jnp.float32),
            pltpu.VMEM((tokens, width), jnp.bfloat16),
            pltpu.VMEM((tokens, channels), jnp.bfloat16),
            pltpu.VMEM((tokens, channels), jnp.bfloat16),
            pltpu.VMEM((tokens, channels), jnp.float32),
            pltpu.VMEM((count, share, LANES), jnp.bfloat16),
            pltpu.VMEM((count, share, LANES), jnp.bfloat16),
            pltpu.VMEM((count, share, LANES), jnp.bfloat16),
            pltpu.VMEM((count, share, LANES), jnp.bfloat16),
            pltpu.VMEM((HALVES * away, tokens // HALVES, tile), jnp.bfloat16),
            pltpu.VMEM((HALVES * away, tokens // HALVES, tile), jnp.bfloat16),
            pltpu.VMEM((each // tile, tokens, tile), jnp.float32),
            pltpu.SemaphoreType.DMA((tiles,)),
        ]
        + [pltpu.SemaphoreType.DMA((count,))] * 4
        + [pltpu.SemaphoreType.DMA((HALVES * away,))] * 2,
        compiler_params=pltpu.CompilerParams(
            vmem_limit_bytes=61 * 2**20, collective_id=0, has_side_effects=True
        ),
        name="layer",
    )(
        projected, halo, short_weight, rate_b, residue_b, skip[None],
        rate_b.reshape(count, share, LANES), fwd, inv, w_out,
    )


def solution(mesh):
    return jax.shard_map(
        on_device,
        mesh=mesh,
        in_specs=(
            P(None, "ctx", "tp"),
            P(None, None, "tp"),
            P("tp", None),
            P("tp", None),
            P("tp"),
            P("tp", None),
        ),
        out_specs=P("ctx", "tp"),
        check_vma=False,
    )
```

```python
import math

import jax
import jax.numpy as jnp
import numpy as np
from jax import lax
from jax.experimental import pallas as pl
from jax.experimental.pallas import tpu as pltpu
from jax.sharding import PartitionSpec as P

LANES = 128
SUB = 8
SPAN = 4
HALVES = 2
MESH = pl.DeviceIdType.MESH


def half_tables(block):
    k = np.arange(block)[:, None]
    t = np.arange(block)[None, :]
    angle = np.pi / (2 * block) * ((2 * k + 1) * t % (4 * block))
    fwd = np.concatenate([np.cos(angle), np.sin(angle)], axis=0)
    return jnp.asarray(fwd, jnp.bfloat16), jnp.asarray(fwd.T, jnp.bfloat16)


def spread(rows):
    return jnp.stack(
        [jnp.broadcast_to(rows[m : m + 1], (SUB, LANES)) for m in range(rows.shape[0])]
    )


def mode_weight(rates, residues, modes):
    return residues * jnp.sqrt(2.0 * rates / modes)


def fold(power):
    while power.shape[0] > 1 and power.shape[0] % 2 == 0:
        half = power.shape[0] // 2
        power = power[:half] + power[half:]
    return jnp.sum(power, axis=0)


def layer_kernel(
    halo, short, rate, residue, skip, fwd, inv, proj_hbm, w_out, out,
    proj, w_buf, line, taps, prod, query, base, state, got, enter_out, enter, send, recv, own,
    p_sem, w_sem, s1, r1, s2, r2, s3, r3,
):
    _, tokens, channels = proj.shape
    modes = rate.shape[0]
    count, share = got.shape[0], got.shape[1]
    parts, rank = lax.axis_size("tp"), lax.axis_index("ctx")
    me = lax.axis_index("tp")
    tiles, _, tile = w_buf.shape
    per = tiles // parts
    away = tiles - per
    width = taps.shape[1]
    group = SPAN * SUB
    row = lax.broadcasted_iota(jnp.int32, (1, SUB, LANES), 1).astype(jnp.float32)

    def load(i):
        peer = lax.rem(me + 1 + i // per, parts)
        col = pl.multiple_of((peer * per + i % per) * tile, tile)
        return pltpu.make_async_copy(w_out.at[:, pl.ds(col, tile)], w_buf.at[i], w_sem.at[i])

    chunks = p_sem.shape[0]
    chunk = channels // chunks

    def fetch(c):
        cols = pl.ds(c * chunk, chunk)
        return pltpu.make_async_copy(proj_hbm.at[:, :, cols], proj.at[:, :, cols], p_sem.at[c])

    for c in range(chunks):
        fetch(c).start()

    @pl.loop(0, tiles)
    def _(i):
        load(i).start()

    barrier = pltpu.get_barrier_semaphore()

    @pl.loop(1, count)
    def _(o):
        pl.semaphore_signal(
            barrier, inc=1, device_id=(lax.rem(rank + o, count), me), device_id_type=MESH
        )

    @pl.loop(1, parts)
    def _(o):
        pl.semaphore_signal(
            barrier, inc=1, device_id=(rank, lax.rem(me + o, parts)), device_id_type=MESH
        )

    def features(j):
        lanes = pl.ds(pl.multiple_of(j * LANES, LANES), LANES)
        feats = []
        for s in range(3):
            now = proj[s, :, lanes].astype(jnp.float32)
            line[s, SUB - 2 : SUB, :] = halo[s, :, lanes].astype(jnp.float32)
            line[s, SUB : SUB + tokens, :] = now
            mixed = (
                short[s, 0:1, lanes] * now
                + short[s, 1:2, lanes] * line[s, SUB - 1 : SUB - 1 + tokens, :]
                + short[s, 2:3, lanes] * line[s, SUB - 2 : SUB - 2 + tokens, :]
            )
            feats.append(mixed.astype(jnp.bfloat16))
        query[:, lanes] = feats[0]
        product = (feats[1].astype(jnp.float32) * feats[2].astype(jnp.float32)).astype(jnp.bfloat16)
        prod[:, lanes] = product
        line[0, SUB : SUB + tokens, :] = product.astype(jnp.float32)
        rates = spread(rate[:, lanes])
        step = jnp.exp(-SUB * rates)

        def advance(i, held):
            for k in range(SPAN):
                start = pl.multiple_of(SUB + i * group + k * SUB, SUB)
                held = held * step + line[0, pl.ds(start, SUB), :][None]
            return held

        held = lax.fori_loop(0, tokens // group, advance, jnp.zeros((modes, SUB, LANES), jnp.float32))
        held = jnp.sum(held * jnp.exp(-rates * (SUB - 1 - row)), axis=1).astype(state.dtype)
        if share >= modes:
            times = share // modes
            at = pl.multiple_of((j % times) * modes, modes)
            state[j // times, pl.ds(at, modes), :] = held
        else:
            times = modes // share
            for i in range(times):
                state[j * times + i] = held[i * share : (i + 1) * share]

    for c in range(chunks):
        fetch(c).wait()
        pl.loop(c * (chunk // LANES), (c + 1) * (chunk // LANES))(features)

    pl.semaphore_wait(barrier, count + parts - 2)

    def inside(start, stop):
        @pl.loop(start, stop)
        def _(b):
            cols = pl.ds(pl.multiple_of(b * width, width), width)
            for n in range(width // LANES):
                j = b * (width // LANES) + n
                lanes = pl.ds(pl.multiple_of(j * LANES, LANES), LANES)
                rates = spread(rate[:, lanes])
                weight = mode_weight(rates, spread(residue[:, lanes]), modes)
                step = jnp.exp(-SUB * rates)

                def advance(i, power):
                    rows = []
                    for _ in range(SPAN):
                        rows.append(fold(power))
                        power = power * step
                    at = pl.ds(pl.multiple_of(i * group, group), group)
                    taps[at, n * LANES : (n + 1) * LANES] = jnp.concatenate(rows, axis=0).astype(
                        jnp.bfloat16
                    )
                    return power

                lax.fori_loop(0, tokens // group, advance, weight * jnp.exp(-rates * row))
            here = prod[:, cols]
            sig = jnp.dot(fwd[...], here, preferred_element_type=jnp.float32)
            fil = jnp.dot(fwd[...], taps[...], preferred_element_type=jnp.float32)
            cs, ss, cf, sf = sig[:tokens], sig[tokens:], fil[:tokens], fil[tokens:]
            both = jnp.concatenate(
                [
                    (cs * cf - ss * sf).astype(jnp.bfloat16),
                    (cs * sf + ss * cf).astype(jnp.bfloat16),
                ],
                axis=0,
            )
            conv = jnp.dot(inv[...], both, preferred_element_type=jnp.float32) * (1.0 / tokens)
            base[:, cols] = conv + skip[:, cols] * here.astype(jnp.float32)

    pieces = channels // width
    def hop(src, dst, peer, slot, sent, landed):
        return pltpu.make_async_remote_copy(
            src_ref=src.at[peer], dst_ref=dst.at[slot], send_sem=sent.at[peer],
            recv_sem=landed.at[slot], device_id=(peer, me), device_id_type=MESH,
        )

    @pl.loop(1, count)
    def _(o):
        hop(state, got, lax.rem(rank + o, count), rank, s1, r1).start()

    got[rank] = state[rank]
    inside(0, pieces // 2)

    @pl.loop(1, count)
    def _(o):
        peer = lax.rem(rank + o, count)
        hop(state, got, peer, peer, s1, r1).wait()

    if share >= modes:
        own_rate = jnp.concatenate(
            [
                rate[:, pl.ds(pl.multiple_of((rank * (share // modes) + i) * LANES, LANES), LANES)]
                for i in range(share // modes)
            ],
            axis=0,
        )
    else:
        times = modes // share
        at = pl.multiple_of((rank // times) * LANES, LANES)
        column = rate[:, pl.ds(at, LANES)]
        own_rate = column[:share]
        for i in range(1, times):
            own_rate = jnp.where(
                rank % times == i, column[i * share : (i + 1) * share], own_rate
            )
    decay = jnp.exp(-float(tokens) * own_rate)

    def prefix(i, held):
        enter_out[i] = held.astype(enter_out.dtype)
        return held * decay + got[i].astype(jnp.float32)

    lax.fori_loop(0, count, prefix, jnp.zeros((share, LANES), jnp.float32))

    @pl.loop(1, count)
    def _(o):
        hop(enter_out, enter, lax.rem(rank + o, count), rank, s2, r2).start()

    enter[rank] = enter_out[rank]
    inside(pieces // 2, pieces)

    @pl.loop(1, count)
    def _(o):
        peer = lax.rem(rank + o, count)
        hop(enter_out, enter, peer, peer, s2, r2).wait()

    def entering(j):
        if share >= modes:
            times = share // modes
            at = pl.multiple_of((j % times) * modes, modes)
            return spread(enter[j // times, pl.ds(at, modes), :].astype(jnp.float32))
        times = modes // share
        return jnp.concatenate(
            [spread(enter[j * times + i].astype(jnp.float32)) for i in range(times)], axis=0
        )

    part = tokens // HALVES

    def gate(begin):
        @pl.loop(0, channels // LANES)
        def _(j):
            lanes = pl.ds(pl.multiple_of(j * LANES, LANES), LANES)
            rates = spread(rate[:, lanes])
            weight = mode_weight(rates, spread(residue[:, lanes]), modes)
            step = jnp.exp(-SUB * rates)

            def advance(i, power):
                rows = []
                for _ in range(SPAN):
                    rows.append(fold(power))
                    power = power * step
                at = pl.ds(pl.multiple_of(begin + i * group, group), group)
                total = jnp.concatenate(rows, axis=0) + base[at, lanes]
                query[at, lanes] = (query[at, lanes].astype(jnp.float32) * total).astype(
                    jnp.bfloat16
                )
                return power

            lax.fori_loop(
                0, part // group, advance,
                weight * jnp.exp(-rates * (row + (begin + 1.0))) * entering(j),
            )

    def give(i):
        peer = lax.rem(me + 1 + (i % away) // per, parts)
        return pltpu.make_async_remote_copy(
            src_ref=send.at[i], dst_ref=recv.at[i], send_sem=s3.at[i], recv_sem=r3.at[i],
            device_id=(rank, peer), device_id_type=MESH,
        )

    for h in range(HALVES):
        gate(h * part)

        @pl.loop(0, away)
        def _(i):
            if h == 0:
                load(i).wait()
            send[h * away + i] = jnp.dot(
                query[h * part : (h + 1) * part, :], w_buf[i], preferred_element_type=jnp.float32
            ).astype(jnp.bfloat16)
            give(h * away + i).start()

    @pl.loop(0, per)
    def _(t):
        load(away + t).wait()
        own[t] = jnp.dot(query[...], w_buf[away + t], preferred_element_type=jnp.float32)

    for h in range(HALVES):
        for t in range(per):
            total = own[t, h * part : (h + 1) * part, :]
            for o in range(parts - 1):
                give(h * away + o * per + t).wait()
                total = total + recv[h * away + o * per + t].astype(jnp.float32)
            out[h * part : (h + 1) * part, t * tile : (t + 1) * tile] = total.astype(out.dtype)


def on_device(projected, short_weight, rate, residue, skip, w_out):
    count = lax.axis_size("ctx")
    parts = lax.axis_size("tp")
    _, tokens, channels = projected.shape
    modes = rate.shape[1]
    outputs = w_out.shape[1]
    blocks = channels // LANES
    halo = lax.ppermute(
        projected[:, -2:, :], "ctx", [(i, i + 1) for i in range(count - 1)]
    )
    fwd, inv = half_tables(tokens)
    width = min(512, channels)
    share = blocks * modes // count
    each = outputs // parts
    tile = min(512, each)
    tiles = outputs // tile
    away = tiles - each // tile
    vmem = pl.BlockSpec(memory_space=pltpu.VMEM)
    return pl.pallas_call(
        layer_kernel,
        in_specs=[vmem] * 7 + [pl.BlockSpec(memory_space=pl.ANY)] * 2,
        out_specs=vmem,
        out_shape=jax.ShapeDtypeStruct((tokens, each), jnp.bfloat16),
        scratch_shapes=[
            pltpu.VMEM(projected.shape, jnp.bfloat16),
            pltpu.VMEM((tiles, channels, tile), jnp.bfloat16),
            pltpu.VMEM((3, tokens + SUB, LANES), jnp.float32),
            pltpu.VMEM((tokens, width), jnp.bfloat16),
            pltpu.VMEM((tokens, channels), jnp.bfloat16),
            pltpu.VMEM((tokens, channels), jnp.bfloat16),
            pltpu.VMEM((tokens, channels), jnp.float32),
            pltpu.VMEM((count, share, LANES), jnp.bfloat16),
            pltpu.VMEM((count, share, LANES), jnp.bfloat16),
            pltpu.VMEM((count, share, LANES), jnp.bfloat16),
            pltpu.VMEM((count, share, LANES), jnp.bfloat16),
            pltpu.VMEM((HALVES * away, tokens // HALVES, tile), jnp.bfloat16),
            pltpu.VMEM((HALVES * away, tokens // HALVES, tile), jnp.bfloat16),
            pltpu.VMEM((each // tile, tokens, tile), jnp.float32),
            pltpu.SemaphoreType.DMA((channels // width,)),
            pltpu.SemaphoreType.DMA((tiles,)),
        ]
        + [pltpu.SemaphoreType.DMA((count,))] * 4
        + [pltpu.SemaphoreType.DMA((HALVES * away,))] * 2,
        compiler_params=pltpu.CompilerParams(
            vmem_limit_bytes=61 * 2**20, collective_id=0, has_side_effects=True
        ),
        name="layer",
    )(
        halo, short_weight, rate.T, residue.T, skip[None], fwd, inv, projected, w_out,
    )


def solution(mesh):
    return jax.shard_map(
        on_device,
        mesh=mesh,
        in_specs=(
            P(None, "ctx", "tp"),
            P(None, None, "tp"),
            P("tp", None),
            P("tp", None),
            P("tp"),
            P("tp", None),
        ),
        out_specs=P("ctx", "tp"),
        check_vma=False,
    )
```
